32 devices in a mesh: section: 4 (over x, core), dp: 8 (over z, y).
Axes of the slice: x: 2, y: 2, z: 4, core: 2. Of those that a mesh axis runs over, the one named last changes fastest.
Arguments:
- layer_inputs: bfloat16 [4, 8, 512, 4096], P('section', 'dp'), may hold values from -6 to 6
- out_grads: bfloat16 [4, 8, 512, 4096], P('section', 'dp'), may hold values from -6 to 6
- projections: bfloat16 [4, 4096, 128], P('section'), may hold values from -0.09375 to 0.09375
- query_grads: bfloat16 [4, 256, 4096], P('section', 'dp'), may hold values from -0.59765625 to 0.59765625
- lengths: int32 [8], P('dp'), may hold values from 1 to 512, as said below
Outputs:
- scores: float32 [8, 256], P('dp', 'section')
The draws below stay inside these ranges and needn't reach their ends.
Inputs may be any that keep to these rules, and one draw needn't show every extreme that they name: `lengths`: some training example fills all 512 slots.
All inputs are finite; a program needn't handle non-finite values.
Results may differ from the reference program's by a relative error of at most 0.005.
Values may be sent and summed in bfloat16 or wider, within the bound.
A program may use at most 128 MiB of HBM per device.

```python
import jax
import jax.numpy as jnp

D = 4096
RANK = 64
SEQ = 512
LAYERS = 4
EX = 8
QUERIES = 256


def draw_lengths(key, part):
    drawn = jax.random.randint(jax.random.fold_in(key, 11), (EX,), 1, SEQ + 1)
    full_slot = jax.random.randint(jax.random.fold_in(key, 12), (), 0, EX)
    return jnp.where(jnp.arange(EX) == full_slot, SEQ, drawn).astype(jnp.int32)


def levels(own_key, dims, split, low, top_value):
    gain, own = 1.0, jax.random.fold_in(own_key, 6)
    for dim, shards_of in split:
        steps = jnp.exp(jax.random.uniform(jax.random.fold_in(own, dim), (shards_of,), jnp.float32, low / len(split), top_value / len(split)))
        gain = gain * jnp.repeat(steps, dims[dim] // shards_of).reshape([-1 if axis == dim else 1 for axis in range(len(dims))])
    return gain


def scatter_about(stream_key, shape, width, bound, cuts=(), kind=jnp.bfloat16):
    result = jax.random.normal(stream_key, shape, jnp.float32) * width
    if len(cuts) > 0:
        result = levels(stream_key, shape, cuts, -0.22, 0.18) * result
    return jnp.clip(result, min=-bound, max=bound).astype(kind)


def setup_inputs(seed: int = 0) -> dict:
    seeds = jax.random.split(jax.random.key(seed), 6)
    layer_inputs = scatter_about(seeds[0], (LAYERS, EX, SEQ, D), 1.0, 6.0, ((0, 4), (1, 8)))
    out_grads = scatter_about(seeds[1], (LAYERS, EX, SEQ, D), 1.0, 6.0, ((0, 4), (1, 8)))
    projections = scatter_about(seeds[2], (LAYERS, D, 2 * RANK), D ** -0.5, 0.09375, ((0, 4),))
    query_grads = scatter_about(seeds[3], (LAYERS, QUERIES, RANK * RANK), 0.1, 0.59765625, ((0, 4), (1, 8)))
    lengths = draw_lengths(jax.random.fold_in(seeds[5], 71), 0)
    return {"layer_inputs": layer_inputs, "out_grads": out_grads, "projections": projections, "query_grads": query_grads, "lengths": lengths}


def reference(layer_inputs, out_grads, projections, query_grads, lengths):
    valid_mask = (jnp.arange(SEQ)[None, :] < lengths[:, None]).astype(jnp.float32)
    token_count = lengths.astype(jnp.float32)
    score_total = jnp.zeros((EX, QUERIES), jnp.float32)
    for layer_index in range(LAYERS):
        flat_in = layer_inputs[layer_index].reshape(EX * SEQ, D)
        flat_grad = out_grads[layer_index].reshape(EX * SEQ, D)
        proj_table = projections[layer_index]
        input_side = jnp.dot(flat_in, proj_table[:, :RANK], preferred_element_type=jnp.float32).astype(jnp.bfloat16).reshape(EX, SEQ, RANK)
        grad_side = jnp.dot(flat_grad, proj_table[:, RANK:], preferred_element_type=jnp.float32).astype(jnp.bfloat16).reshape(EX, SEQ, RANK)
        masked = grad_side.astype(jnp.float32) * valid_mask[:, :, None]
        example = jnp.einsum("esa,esb->eab", masked, input_side.astype(jnp.float32)) / token_count[:, None, None]
        example = example.astype(jnp.bfloat16).reshape(EX, RANK * RANK)
        score_total = score_total + jnp.dot(example, query_grads[layer_index].T, preferred_element_type=jnp.float32)
    return score_total
```

```python
import functools

import jax
import jax.numpy as jnp
from jax import lax
from jax.experimental import pallas as pl
from jax.experimental.pallas import tpu as pltpu
from jax.sharding import PartitionSpec as P

MESH = pl.DeviceIdType.MESH
CHUNKS = 4


def kernel(
    sections, members, width,
    inputs_ref, grads_ref, proj_ref, query_ref, length_ref, out_ref,
    rows, proj, query, length, product, packed, spread, scores, parts,
    row_sem, proj_sem, query_sem, length_sem,
    grad_send, grad_recv, score_send, score_recv,
):
    sec, dp = lax.axis_index("section"), lax.axis_index("dp")
    seq_len = inputs_ref.shape[2]
    step = seq_len // CHUNKS
    rank = proj_ref.shape[2] // 2
    block = query_ref.shape[1]
    group = members // sections
    per = width // block
    home = dp // group
    keeps = home == sec
    my_slot = (dp % group) // per * (sections * per) + sec * per + dp % per

    length_copy = pltpu.make_async_copy(length_ref, length, length_sem)
    length_copy.start()
    proj_copy = pltpu.make_async_copy(proj_ref.at[0], proj, proj_sem)
    proj_copy.start()
    row_copies = []
    for c in range(CHUNKS):
        span = pl.ds(c * step, step)
        pair = (
            pltpu.make_async_copy(inputs_ref.at[0, 0, span], rows.at[c, pl.ds(0, step)], row_sem.at[c, 0]),
            pltpu.make_async_copy(grads_ref.at[0, 0, span], rows.at[c, pl.ds(step, step)], row_sem.at[c, 1]),
        )
        for copy in pair:
            copy.start()
        row_copies.append(pair)
    query_copies = []
    for k in range(per):
        copy = pltpu.make_async_copy(query_ref.at[0], query.at[pl.ds(k * block, block)], query_sem.at[k])
        copy.start()
        query_copies.append(copy)

    barrier = pltpu.get_barrier_semaphore()

    @pl.loop(1, members)
    def _(k):
        pl.semaphore_signal(
            barrier, inc=1, device_id=(sec, lax.rem(dp + k, members)), device_id_type=MESH
        )

    @pl.loop(0, sections)
    def _(s):
        @pl.loop(0, group)
        def _(g):
            sender = sec * group + g

            @pl.when(jnp.logical_not(jnp.logical_and(s == sec, sender == dp)))
            def _():
                pl.semaphore_signal(barrier, inc=1, device_id=(s, sender), device_id_type=MESH)

    length_copy.wait()
    proj_copy.wait()
    tokens = length[0]
    total = jnp.zeros((2 * rank, 2 * rank), jnp.float32)
    for c in range(CHUNKS):
        for copy in row_copies[c]:
            copy.wait()
        sides = jnp.dot(rows[c], proj[...], preferred_element_type=jnp.float32).astype(jnp.bfloat16)
        slot = lax.broadcasted_iota(jnp.int32, (step, 2 * rank), 0) + c * step
        masked = jnp.where(slot < tokens, sides[step:].astype(jnp.float32), 0.0).astype(jnp.bfloat16)
        total += lax.dot_general(
            masked, sides[:step], (((0,), (0,)), ((), ())), preferred_element_type=jnp.float32
        )
    product[...] = total[rank:]
    half = rank // 2
    even = product[pl.ds(0, half, stride=2), :]
    odd = product[pl.ds(1, half, stride=2), :]
    lane = lax.broadcasted_iota(jnp.int32, (half, 2 * rank), 1)
    folded = jnp.where(lane < rank, even, pltpu.roll(odd, rank, 1))
    packed[dp] = (folded / tokens.astype(jnp.float32)).astype(jnp.bfloat16)

    pl.semaphore_wait(barrier, members - 1 + sections * group - jnp.where(keeps, 1, 0))

    def grad_copy(k):
        return pltpu.make_async_remote_copy(
            src_ref=packed.at[dp], dst_ref=packed.at[dp],
            send_sem=grad_send.at[k], recv_sem=grad_recv.at[k],
            device_id=(sec, lax.rem(dp + k, members)), device_id_type=MESH,
        )

    @pl.loop(1, members)
    def _(k):
        grad_copy(k).start()

    for copy in query_copies:
        copy.wait()

    @pl.loop(1, members)
    def _(k):
        grad_copy(k).wait_recv()

    spread[...] = packed[...].reshape(members * half, 2 * rank).astype(jnp.float32)
    left = jnp.concatenate(
        [spread[pl.ds(i, members, stride=half), :].astype(jnp.bfloat16) for i in range(half)], axis=1
    )
    found = lax.dot_general(
        left, query[...], (((1,), (1,)), ((), ())), preferred_element_type=jnp.float32
    )
    place = lax.broadcasted_iota(jnp.int32, found.shape, 1) // block
    found = jnp.where(place == dp % per, found, 0.0)
    scores[...] = found.reshape(members, 1, width)

    def score_copy(e):
        return pltpu.make_async_remote_copy(
            src_ref=scores.at[e], dst_ref=parts.at[my_slot],
            send_sem=score_send.at[e], recv_sem=score_recv.at[my_slot],
            device_id=(home, e), device_id_type=MESH,
        )

    @pl.loop(0, members)
    def _(k):
        e = lax.rem(dp + k, members)

        @pl.when(jnp.logical_or(jnp.logical_not(keeps), k > 0))
        def _():
            score_copy(e).start()

    @pl.when(keeps)
    def _():
        parts[my_slot] = scores[dp]

    @pl.loop(0, sections * group)
    def _(slot):
        @pl.when(jnp.logical_or(jnp.logical_not(keeps), slot != my_slot))
        def _():
            pltpu.make_async_remote_copy(
                src_ref=scores.at[0], dst_ref=parts.at[slot],
                send_sem=score_send.at[0], recv_sem=score_recv.at[slot],
                device_id=(home, dp), device_id_type=MESH,
            ).wait_recv()

    count = sections * per
    for b in range(group // per):
        piece = parts[b * count]
        for k in range(1, count):
            piece = piece + parts[b * count + k]
        out_ref[:, pl.ds(b * width, width)] = piece

    @pl.loop(1, members)
    def _(k):
        grad_copy(k).wait_send()

    @pl.loop(0, members)
    def _(k):
        @pl.when(jnp.logical_or(jnp.logical_not(keeps), k > 0))
        def _():
            score_copy(lax.rem(dp + k, members)).wait_send()


def solution(mesh):
    sections, members = mesh.shape["section"], mesh.shape["dp"]

    def on_device(layer_inputs, out_grads, projections, query_grads, lengths):
        seq_len, model_width = layer_inputs.shape[2:]
        rank = projections.shape[2] // 2
        block = query_grads.shape[1]
        flat = query_grads.shape[2]
        group = members // sections
        width = min(128, block * group)
        per = width // block
        half = rank // 2
        slots = sections * group
        step = seq_len // CHUNKS
        return pl.pallas_call(
            functools.partial(kernel, sections, members, width),
            out_shape=jax.ShapeDtypeStruct((1, block * group), jnp.float32),
            in_specs=[pl.BlockSpec(memory_space=pltpu.HBM)] * 5,
            out_specs=pl.BlockSpec(memory_space=pltpu.VMEM),
            scratch_shapes=[
                pltpu.VMEM((CHUNKS, 2 * step, model_width), jnp.bfloat16),
                pltpu.VMEM((model_width, 2 * rank), jnp.bfloat16),
                pltpu.VMEM((width, flat), jnp.bfloat16),
                pltpu.SMEM((1,), jnp.int32),
                pltpu.VMEM((rank, 2 * rank), jnp.float32),
                pltpu.VMEM((members, half, 2 * rank), jnp.bfloat16),
                pltpu.VMEM((members * half, 2 * rank), jnp.float32),
                pltpu.VMEM((members, 1, width), jnp.float32),
                pltpu.VMEM((slots, 1, width), jnp.float32),
                pltpu.SemaphoreType.DMA((CHUNKS, 2)),
                pltpu.SemaphoreType.DMA,
                pltpu.SemaphoreType.DMA((per,)),
                pltpu.SemaphoreType.DMA,
                pltpu.SemaphoreType.DMA((members,)),
                pltpu.SemaphoreType.DMA((members,)),
                pltpu.SemaphoreType.DMA((members,)),
                pltpu.SemaphoreType.DMA((slots,)),
            ],
            compiler_params=pltpu.CompilerParams(
                collective_id=0, has_side_effects=True, vmem_limit_bytes=48 * 1024 * 1024
            ),
            cost_estimate=pl.CostEstimate(
                flops=8 * seq_len * model_width * rank,
                bytes_accessed=4 * seq_len * model_width,
                transcendentals=0,
            ),
        )(layer_inputs, out_grads, projections, query_grads, lengths)

    placed = (
        P("section", "dp", None, None),
        P("section", "dp", None, None),
        P("section", None, None),
        P("section", "dp", None),
        P("dp"),
    )
    return jax.shard_map(
        on_device, mesh=mesh, in_specs=placed, out_specs=P("dp", "section"), check_vma=False
    )
```

```python
import functools

import jax
import jax.numpy as jnp
from jax import lax
from jax.experimental import pallas as pl
from jax.experimental.pallas import tpu as pltpu
from jax.sharding import PartitionSpec as P

MESH = pl.DeviceIdType.MESH
CHUNKS = 4


def kernel(
    sections, members, width,
    inputs_ref, grads_ref, proj_ref, query_ref, length_ref, out_ref,
    rows, proj, query, product, packed, spread, scores, parts,
    row_sem, proj_sem, query_sem,
    grad_send, grad_recv, score_send, score_recv,
):
    sec, dp = lax.axis_index("section"), lax.axis_index("dp")
    seq_len = inputs_ref.shape[2]
    step = seq_len // CHUNKS
    rank = proj_ref.shape[2] // 2
    block = query_ref.shape[1]
    group = members // sections
    per = width // block
    home = dp // group
    keeps = home == sec
    my_slot = (dp % group) // per * (sections * per) + sec * per + dp % per

    proj_copy = pltpu.make_async_copy(proj_ref.at[0], proj, proj_sem)
    proj_copy.start()
    row_copies = []
    for c in range(CHUNKS):
        span = pl.ds(c * step, step)
        pair = (
            pltpu.make_async_copy(inputs_ref.at[0, 0, span], rows.at[c, pl.ds(0, step)], row_sem.at[c, 0]),
            pltpu.make_async_copy(grads_ref.at[0, 0, span], rows.at[c, pl.ds(step, step)], row_sem.at[c, 1]),
        )
        for copy in pair:
            copy.start()
        row_copies.append(pair)
    query_copies = []
    for k in range(per):
        copy = pltpu.make_async_copy(query_ref.at[0], query.at[pl.ds(k * block, block)], query_sem.at[k])
        copy.start()
        query_copies.append(copy)

    barrier = pltpu.get_barrier_semaphore()

    @pl.loop(1, members)
    def _(k):
        pl.semaphore_signal(
            barrier, inc=1, device_id=(sec, lax.rem(dp + k, members)), device_id_type=MESH
        )

    @pl.loop(0, sections)
    def _(s):
        @pl.loop(0, group)
        def _(g):
            sender = sec * group + g

            @pl.when(jnp.logical_not(jnp.logical_and(s == sec, sender == dp)))
            def _():
                pl.semaphore_signal(barrier, inc=1, device_id=(s, sender), device_id_type=MESH)

    proj_copy.wait()
    tokens = length_ref[0]
    total = jnp.zeros((2 * rank, 2 * rank), jnp.float32)
    for c in range(CHUNKS):
        for copy in row_copies[c]:
            copy.wait()
        sides = jnp.dot(rows[c], proj[...], preferred_element_type=jnp.float32).astype(jnp.bfloat16)
        slot = lax.broadcasted_iota(jnp.int32, (step, 2 * rank), 0) + c * step
        masked = jnp.where(slot < tokens, sides[step:].astype(jnp.float32), 0.0).astype(jnp.bfloat16)
        total += lax.dot_general(
            masked, sides[:step], (((0,), (0,)), ((), ())), preferred_element_type=jnp.float32
        )
    product[...] = total[rank:]
    half = rank // 2
    even = product[pl.ds(0, half, stride=2), :]
    odd = product[pl.ds(1, half, stride=2), :]
    lane = lax.broadcasted_iota(jnp.int32, (half, 2 * rank), 1)
    folded = jnp.where(lane < rank, even, pltpu.roll(odd, rank, 1))
    packed[dp] = (folded / tokens.astype(jnp.float32)).astype(jnp.bfloat16)

    pl.semaphore_wait(barrier, members - 1 + sections * group - jnp.where(keeps, 1, 0))

    def grad_copy(k):
        return pltpu.make_async_remote_copy(
            src_ref=packed.at[dp], dst_ref=packed.at[dp],
            send_sem=grad_send.at[k], recv_sem=grad_recv.at[k],
            device_id=(sec, lax.rem(dp + k, members)), device_id_type=MESH,
        )

    @pl.loop(1, members)
    def _(k):
        grad_copy(k).start()

    for copy in query_copies:
        copy.wait()

    @pl.loop(1, members)
    def _(k):
        grad_copy(k).wait_recv()

    spread[...] = packed[...].reshape(members * half, 2 * rank).astype(jnp.float32)
    left = jnp.concatenate(
        [spread[pl.ds(i, members, stride=half), :].astype(jnp.bfloat16) for i in range(half)], axis=1
    )
    found = lax.dot_general(
        left, query[...], (((1,), (1,)), ((), ())), preferred_element_type=jnp.float32
    )
    place = lax.broadcasted_iota(jnp.int32, found.shape, 1) // block
    found = jnp.where(place == dp % per, found, 0.0)
    scores[...] = found.reshape(members, 1, width)

    def score_copy(e):
        return pltpu.make_async_remote_copy(
            src_ref=scores.at[e], dst_ref=parts.at[my_slot],
            send_sem=score_send.at[e], recv_sem=score_recv.at[my_slot],
            device_id=(home, e), device_id_type=MESH,
        )

    @pl.loop(0, members)
    def _(k):
        e = lax.rem(dp + k, members)

        @pl.when(jnp.logical_or(jnp.logical_not(keeps), k > 0))
        def _():
            score_copy(e).start()

    @pl.when(keeps)
    def _():
        parts[my_slot] = scores[dp]

    @pl.loop(0, sections * group)
    def _(slot):
        @pl.when(jnp.logical_or(jnp.logical_not(keeps), slot != my_slot))
        def _():
            pltpu.make_async_remote_copy(
                src_ref=scores.at[0], dst_ref=parts.at[slot],
                send_sem=score_send.at[0], recv_sem=score_recv.at[slot],
                device_id=(home, dp), device_id_type=MESH,
            ).wait_recv()

    count = sections * per
    for b in range(group // per):
        piece = parts[b * count]
        for k in range(1, count):
            piece = piece + parts[b * count + k]
        out_ref[:, pl.ds(b * width, width)] = piece

    @pl.loop(1, members)
    def _(k):
        grad_copy(k).wait_send()

    @pl.loop(0, members)
    def _(k):
        @pl.when(jnp.logical_or(jnp.logical_not(keeps), k > 0))
        def _():
            score_copy(lax.rem(dp + k, members)).wait_send()


def solution(mesh):
    sections, members = mesh.shape["section"], mesh.shape["dp"]

    def on_device(layer_inputs, out_grads, projections, query_grads, lengths):
        seq_len, model_width = layer_inputs.shape[2:]
        rank = projections.shape[2] // 2
        block = query_grads.shape[1]
        flat = query_grads.shape[2]
        group = members // sections
        width = min(128, block * group)
        per = width // block
        half = rank // 2
        slots = sections * group
        step = seq_len // CHUNKS
        return pl.pallas_call(
            functools.partial(kernel, sections, members, width),
            out_shape=jax.ShapeDtypeStruct((1, block * group), jnp.float32),
            in_specs=[pl.BlockSpec(memory_space=pltpu.HBM)] * 4 + [pl.BlockSpec(memory_space=pltpu.SMEM)],
            out_specs=pl.BlockSpec(memory_space=pltpu.VMEM),
            scratch_shapes=[
                pltpu.VMEM((CHUNKS, 2 * step, model_width), jnp.bfloat16),
                pltpu.VMEM((model_width, 2 * rank), jnp.bfloat16),
                pltpu.VMEM((width, flat), jnp.bfloat16),
                pltpu.VMEM((rank, 2 * rank), jnp.float32),
                pltpu.VMEM((members, half, 2 * rank), jnp.bfloat16),
                pltpu.VMEM((members * half, 2 * rank), jnp.float32),
                pltpu.VMEM((members, 1, width), jnp.float32),
                pltpu.VMEM((slots, 1, width), jnp.float32),
                pltpu.SemaphoreType.DMA((CHUNKS, 2)),
                pltpu.SemaphoreType.DMA,
                pltpu.SemaphoreType.DMA((per,)),
                pltpu.SemaphoreType.DMA((members,)),
                pltpu.SemaphoreType.DMA((members,)),
                pltpu.SemaphoreType.DMA((members,)),
                pltpu.SemaphoreType.DMA((slots,)),
            ],
            compiler_params=pltpu.CompilerParams(
                collective_id=0, has_side_effects=True, vmem_limit_bytes=64 * 1024 * 1024
            ),
            cost_estimate=pl.CostEstimate(
                flops=8 * seq_len * model_width * rank,
                bytes_accessed=4 * seq_len * model_width,
                transcendentals=0,
            ),
        )(layer_inputs, out_grads, projections, query_grads, lengths)

    placed = (
        P("section", "dp", None, None),
        P("section", "dp", None, None),
        P("section", None, None),
        P("section", "dp", None),
        P("dp"),
    )
    return jax.shard_map(
        on_device, mesh=mesh, in_specs=placed, out_specs=P("dp", "section"), check_vma=False
    )
```

```python
import functools

import jax
import jax.numpy as jnp
from jax import lax
from jax.experimental import pallas as pl
from jax.experimental.pallas import tpu as pltpu
from jax.sharding import PartitionSpec as P

MESH = pl.DeviceIdType.MESH
CHUNKS = 4


def kernel(
    sections, members, width,
    inputs_ref, grads_ref, proj_ref, query_ref, length_ref, out_ref,
    rows, proj, query, total, packed, spread, scores, parts,
    row_sem, proj_sem, query_sem,
    grad_send, grad_recv, score_send, score_recv,
):
    sec, dp = lax.axis_index("section"), lax.axis_index("dp")
    seq_len = inputs_ref.shape[2]
    step = seq_len // CHUNKS
    rank = proj_ref.shape[2] // 2
    block = query_ref.shape[1]
    group = members // sections
    per = width // block
    home = dp // group
    keeps = home == sec
    my_slot = (dp % group) // per * (sections * per) + sec * per + dp % per

    proj_copy = pltpu.make_async_copy(proj_ref.at[0], proj, proj_sem)
    proj_copy.start()

    def row_copy(c, side, source):
        return pltpu.make_async_copy(
            source.at[0, 0, pl.ds(pl.multiple_of(c * step, step), step)],
            rows.at[c, pl.ds(side * step, step)], row_sem.at[c, side],
        )

    @pl.loop(0, CHUNKS)
    def _(c):
        row_copy(c, 0, inputs_ref).start()
        row_copy(c, 1, grads_ref).start()

    query_copies = []
    for k in range(per):
        copy = pltpu.make_async_copy(query_ref.at[0], query.at[pl.ds(k * block, block)], query_sem.at[k])
        copy.start()
        query_copies.append(copy)

    barrier = pltpu.get_barrier_semaphore()

    @pl.loop(1, members)
    def _(k):
        pl.semaphore_signal(
            barrier, inc=1, device_id=(sec, lax.rem(dp + k, members)), device_id_type=MESH
        )

    @pl.loop(0, sections)
    def _(s):
        @pl.loop(0, group)
        def _(g):
            sender = sec * group + g

            @pl.when(jnp.logical_not(jnp.logical_and(s == sec, sender == dp)))
            def _():
                pl.semaphore_signal(barrier, inc=1, device_id=(s, sender), device_id_type=MESH)

    proj_copy.wait()
    tokens = length_ref[0]
    total[...] = jnp.zeros_like(total)

    @pl.loop(0, CHUNKS)
    def _(c):
        row_copy(c, 0, inputs_ref).wait()
        row_copy(c, 1, grads_ref).wait()
        sides = jnp.dot(rows[c], proj[...], preferred_element_type=jnp.float32).astype(jnp.bfloat16)
        slot = lax.broadcasted_iota(jnp.int32, (step, 2 * rank), 0) + c * step
        masked = jnp.where(slot < tokens, sides[step:].astype(jnp.float32), 0.0).astype(jnp.bfloat16)
        total[...] += lax.dot_general(
            masked, sides[:step], (((0,), (0,)), ((), ())), preferred_element_type=jnp.float32
        )

    half = rank // 2
    even = total[pl.ds(rank, half, stride=2), :]
    odd = total[pl.ds(rank + 1, half, stride=2), :]
    lane = lax.broadcasted_iota(jnp.int32, (half, 2 * rank), 1)
    folded = jnp.where(lane < rank, even, pltpu.roll(odd, rank, 1))
    packed[dp] = (folded / tokens.astype(jnp.float32)).astype(jnp.bfloat16)

    pl.semaphore_wait(barrier, members - 1 + sections * group - jnp.where(keeps, 1, 0))

    def grad_copy(k):
        return pltpu.make_async_remote_copy(
            src_ref=packed.at[dp], dst_ref=packed.at[dp],
            send_sem=grad_send.at[k], recv_sem=grad_recv.at[k],
            device_id=(sec, lax.rem(dp + k, members)), device_id_type=MESH,
        )

    @pl.loop(1, members)
    def _(k):
        grad_copy(k).start()

    for copy in query_copies:
        copy.wait()

    @pl.loop(1, members)
    def _(k):
        grad_copy(k).wait_recv()

    spread[...] = packed[...].reshape(members * half, 2 * rank).astype(jnp.float32)
    left = jnp.concatenate(
        [spread[pl.ds(i, members, stride=half), :].astype(jnp.bfloat16) for i in range(half)], axis=1
    )
    found = lax.dot_general(
        left, query[...], (((1,), (1,)), ((), ())), preferred_element_type=jnp.float32
    )
    place = lax.broadcasted_iota(jnp.int32, found.shape, 1) // block
    found = jnp.where(place == dp % per, found, 0.0)
    scores[...] = found.reshape(members, 1, width)

    def score_copy(e):
        return pltpu.make_async_remote_copy(
            src_ref=scores.at[e], dst_ref=parts.at[my_slot],
            send_sem=score_send.at[e], recv_sem=score_recv.at[my_slot],
            device_id=(home, e), device_id_type=MESH,
        )

    @pl.loop(0, members)
    def _(k):
        e = lax.rem(dp + k, members)

        @pl.when(jnp.logical_or(jnp.logical_not(keeps), k > 0))
        def _():
            score_copy(e).start()

    @pl.when(keeps)
    def _():
        parts[my_slot] = scores[dp]

    @pl.loop(0, sections * group)
    def _(slot):
        @pl.when(jnp.logical_or(jnp.logical_not(keeps), slot != my_slot))
        def _():
            pltpu.make_async_remote_copy(
                src_ref=scores.at[0], dst_ref=parts.at[slot],
                send_sem=score_send.at[0], recv_sem=score_recv.at[slot],
                device_id=(home, dp), device_id_type=MESH,
            ).wait_recv()

    count = sections * per
    for b in range(group // per):
        piece = parts[b * count]
        for k in range(1, count):
            piece = piece + parts[b * count + k]
        out_ref[:, pl.ds(b * width, width)] = piece

    @pl.loop(1, members)
    def _(k):
        grad_copy(k).wait_send()

    @pl.loop(0, members)
    def _(k):
        @pl.when(jnp.logical_or(jnp.logical_not(keeps), k > 0))
        def _():
            score_copy(lax.rem(dp + k, members)).wait_send()


def solution(mesh):
    sections, members = mesh.shape["section"], mesh.shape["dp"]

    def on_device(layer_inputs, out_grads, projections, query_grads, lengths):
        seq_len, model_width = layer_inputs.shape[2:]
        rank = projections.shape[2] // 2
        block = query_grads.shape[1]
        flat = query_grads.shape[2]
        group = members // sections
        width = min(128, block * group)
        per = width // block
        half = rank // 2
        slots = sections * group
        step = seq_len // CHUNKS
        return pl.pallas_call(
            functools.partial(kernel, sections, members, width),
            out_shape=jax.ShapeDtypeStruct((1, block * group), jnp.float32),
            in_specs=[pl.BlockSpec(memory_space=pltpu.HBM)] * 4 + [pl.BlockSpec(memory_space=pltpu.SMEM)],
            out_specs=pl.BlockSpec(memory_space=pltpu.VMEM),
            scratch_shapes=[
                pltpu.VMEM((CHUNKS, 2 * step, model_width), jnp.bfloat16),
                pltpu.VMEM((model_width, 2 * rank), jnp.bfloat16),
                pltpu.VMEM((width, flat), jnp.bfloat16),
                pltpu.VMEM((2 * rank, 2 * rank), jnp.float32),
                pltpu.VMEM((members, half, 2 * rank), jnp.bfloat16),
                pltpu.VMEM((members * half, 2 * rank), jnp.float32),
                pltpu.VMEM((members, 1, width), jnp.float32),
                pltpu.VMEM((slots, 1, width), jnp.float32),
                pltpu.SemaphoreType.DMA((CHUNKS, 2)),
                pltpu.SemaphoreType.DMA,
                pltpu.SemaphoreType.DMA((per,)),
                pltpu.SemaphoreType.DMA((members,)),
                pltpu.SemaphoreType.DMA((members,)),
                pltpu.SemaphoreType.DMA((members,)),
                pltpu.SemaphoreType.DMA((slots,)),
            ],
            compiler_params=pltpu.CompilerParams(
                collective_id=0, has_side_effects=True, vmem_limit_bytes=(64 * 1024 - 128) * 1024
            ),
            cost_estimate=pl.CostEstimate(
                flops=8 * seq_len * model_width * rank,
                bytes_accessed=4 * seq_len * model_width,
                transcendentals=0,
            ),
        )(layer_inputs, out_grads, projections, query_grads, lengths)

    placed = (
        P("section", "dp", None, None),
        P("section", "dp", None, None),
        P("section", None, None),
        P("section", "dp", None),
        P("dp"),
    )
    return jax.shard_map(
        on_device, mesh=mesh, in_specs=placed, out_specs=P("dp", "section"), check_vma=False
    )
```

```python
import functools

import jax
import jax.numpy as jnp
from jax import lax
from jax.experimental import pallas as pl
from jax.experimental.pallas import tpu as pltpu
from jax.sharding import PartitionSpec as P

MESH = pl.DeviceIdType.MESH
CHUNKS = 8


def kernel(
    sections, members, width,
    inputs_ref, grads_ref, proj_ref, query_ref, length_ref, out_ref,
    rows, proj, query, sides, total, packed, spread, scores, parts,
    row_sem, proj_sem, query_sem,
    grad_send, grad_recv, score_send, score_recv,
):
    sec, dp = lax.axis_index("section"), lax.axis_index("dp")
    seq_len = inputs_ref.shape[2]
    step = inputs_ref.shape[3] // CHUNKS
    rank = proj_ref.shape[2] // 2
    block = query_ref.shape[1]
    group = members // sections
    per = width // block
    home = dp // group
    keeps = home == sec
    my_slot = (dp % group) // per * (sections * per) + sec * per + dp % per


    def chunk_copies(c):
        columns = pl.ds(pl.multiple_of(c * step, step), step)
        return (
            pltpu.make_async_copy(proj_ref.at[0, columns], proj.at[c], proj_sem.at[c]),
            pltpu.make_async_copy(
                inputs_ref.at[0, 0, :, columns], rows.at[c, pl.ds(0, seq_len)], row_sem.at[c, 0]
            ),
            pltpu.make_async_copy(
                grads_ref.at[0, 0, :, columns], rows.at[c, pl.ds(seq_len, seq_len)], row_sem.at[c, 1]
            ),
        )

    @pl.loop(0, CHUNKS)
    def _(c):
        for copy in chunk_copies(c):
            copy.start()

    query_copies = []
    for k in range(per):
        copy = pltpu.make_async_copy(query_ref.at[0], query.at[pl.ds(k * block, block)], query_sem.at[k])
        copy.start()
        query_copies.append(copy)

    barrier = pltpu.get_barrier_semaphore()

    @pl.loop(1, members)
    def _(k):
        pl.semaphore_signal(
            barrier, inc=1, device_id=(sec, lax.rem(dp + k, members)), device_id_type=MESH
        )

    @pl.loop(0, sections)
    def _(s):
        @pl.loop(0, group)
        def _(g):
            sender = sec * group + g

            @pl.when(jnp.logical_not(jnp.logical_and(s == sec, sender == dp)))
            def _():
                pl.semaphore_signal(barrier, inc=1, device_id=(s, sender), device_id_type=MESH)

    sides[...] = jnp.zeros_like(sides)

    @pl.loop(0, CHUNKS)
    def _(c):
        for copy in chunk_copies(c):
            copy.wait()
        sides[...] += lax.dot_general(
            proj[c].T, rows[c], (((1,), (1,)), ((), ())), preferred_element_type=jnp.float32
        )

    tokens = length_ref[0]
    slot = lax.broadcasted_iota(jnp.int32, (rank, seq_len), 1)
    grad_side = sides[pl.ds(rank, rank), pl.ds(seq_len, seq_len)]
    total[...] = lax.dot_general(
        jnp.where(slot < tokens, grad_side, 0.0).astype(jnp.bfloat16),
        sides[:, pl.ds(0, seq_len)].astype(jnp.bfloat16),
        (((1,), (1,)), ((), ())), preferred_element_type=jnp.float32,
    )
    half = rank // 2
    even = total[pl.ds(0, half, stride=2), :]
    odd = total[pl.ds(1, half, stride=2), :]
    lane = lax.broadcasted_iota(jnp.int32, (half, 2 * rank), 1)
    folded = jnp.where(lane < rank, even, pltpu.roll(odd, rank, 1))
    packed[dp] = (folded / tokens.astype(jnp.float32)).astype(jnp.bfloat16)

    pl.semaphore_wait(barrier, members - 1 + sections * group - jnp.where(keeps, 1, 0))

    def grad_copy(k):
        return pltpu.make_async_remote_copy(
            src_ref=packed.at[dp], dst_ref=packed.at[dp],
            send_sem=grad_send.at[k], recv_sem=grad_recv.at[k],
            device_id=(sec, lax.rem(dp + k, members)), device_id_type=MESH,
        )

    @pl.loop(1, members)
    def _(k):
        grad_copy(k).start()

    for copy in query_copies:
        copy.wait()

    @pl.loop(1, members)
    def _(k):
        grad_copy(k).wait_recv()

    spread[...] = packed[...].reshape(members * half, 2 * rank).astype(jnp.float32)
    left = jnp.concatenate(
        [spread[pl.ds(i, members, stride=half), :].astype(jnp.bfloat16) for i in range(half)], axis=1
    )
    found = lax.dot_general(
        left, query[...], (((1,), (1,)), ((), ())), preferred_element_type=jnp.float32
    )
    place = lax.broadcasted_iota(jnp.int32, found.shape, 1) // block
    found = jnp.where(place == dp % per, found, 0.0)
    scores[...] = found.reshape(members, 1, width)

    def score_copy(e):
        return pltpu.make_async_remote_copy(
            src_ref=scores.at[e], dst_ref=parts.at[my_slot],
            send_sem=score_send.at[e], recv_sem=score_recv.at[my_slot],
            device_id=(home, e), device_id_type=MESH,
        )

    @pl.loop(0, members)
    def _(k):
        e = lax.rem(dp + k, members)

        @pl.when(jnp.logical_or(jnp.logical_not(keeps), k > 0))
        def _():
            score_copy(e).start()

    @pl.when(keeps)
    def _():
        parts[my_slot] = scores[dp]

    @pl.loop(0, sections * group)
    def _(slot):
        @pl.when(jnp.logical_or(jnp.logical_not(keeps), slot != my_slot))
        def _():
            pltpu.make_async_remote_copy(
                src_ref=scores.at[0], dst_ref=parts.at[slot],
                send_sem=score_send.at[0], recv_sem=score_recv.at[slot],
                device_id=(home, dp), device_id_type=MESH,
            ).wait_recv()

    count = sections * per
    for b in range(group // per):
        piece = parts[b * count]
        for k in range(1, count):
            piece = piece + parts[b * count + k]
        out_ref[:, pl.ds(b * width, width)] = piece

    @pl.loop(1, members)
    def _(k):
        grad_copy(k).wait_send()

    @pl.loop(0, members)
    def _(k):
        @pl.when(jnp.logical_or(jnp.logical_not(keeps), k > 0))
        def _():
            score_copy(lax.rem(dp + k, members)).wait_send()


def solution(mesh):
    sections, members = mesh.shape["section"], mesh.shape["dp"]

    def on_device(layer_inputs, out_grads, projections, query_grads, lengths):
        seq_len, model_width = layer_inputs.shape[2:]
        rank = projections.shape[2] // 2
        block = query_grads.shape[1]
        flat = query_grads.shape[2]
        group = members // sections
        width = min(128, block * group)
        per = width // block
        half = rank // 2
        slots = sections * group
        step = model_width // CHUNKS
        return pl.pallas_call(
            functools.partial(kernel, sections, members, width),
            out_shape=jax.ShapeDtypeStruct((1, block * group), jnp.float32),
            in_specs=[pl.BlockSpec(memory_space=pltpu.HBM)] * 4 + [pl.BlockSpec(memory_space=pltpu.SMEM)],
            out_specs=pl.BlockSpec(memory_space=pltpu.VMEM),
            scratch_shapes=[
                pltpu.VMEM((CHUNKS, 2 * seq_len, step), jnp.bfloat16),
                pltpu.VMEM((CHUNKS, step, 2 * rank), jnp.bfloat16),
                pltpu.VMEM((width, flat), jnp.bfloat16),
                pltpu.VMEM((2 * rank, 2 * seq_len), jnp.float32),
                pltpu.VMEM((rank, 2 * rank), jnp.float32),
                pltpu.VMEM((members, half, 2 * rank), jnp.bfloat16),
                pltpu.VMEM((members * half, 2 * rank), jnp.float32),
                pltpu.VMEM((members, 1, width), jnp.float32),
                pltpu.VMEM((slots, 1, width), jnp.float32),
                pltpu.SemaphoreType.DMA((CHUNKS, 2)),
                pltpu.SemaphoreType.DMA((CHUNKS,)),
                pltpu.SemaphoreType.DMA((per,)),
                pltpu.SemaphoreType.DMA((members,)),
                pltpu.SemaphoreType.DMA((members,)),
                pltpu.SemaphoreType.DMA((members,)),
                pltpu.SemaphoreType.DMA((slots,)),
            ],
            compiler_params=pltpu.CompilerParams(
                collective_id=0, has_side_effects=True, vmem_limit_bytes=(64 * 1024 - 128) * 1024
            ),
            cost_estimate=pl.CostEstimate(
                flops=8 * seq_len * model_width * rank,
                bytes_accessed=4 * seq_len * model_width,
                transcendentals=0,
            ),
        )(layer_inputs, out_grads, projections, query_grads, lengths)

    placed = (
        P("section", "dp", None, None),
        P("section", "dp", None, None),
        P("section", None, None),
        P("section", "dp", None),
        P("dp"),
    )
    return jax.shard_map(
        on_device, mesh=mesh, in_specs=placed, out_specs=P("dp", "section"), check_vma=False
    )
```

```python
import functools

import jax
import jax.numpy as jnp
from jax import lax
from jax.experimental import pallas as pl
from jax.experimental.pallas import tpu as pltpu
from jax.sharding import PartitionSpec as P

MESH = pl.DeviceIdType.MESH
CHUNKS = 8


def kernel(
    sections, members, width,
    inputs_ref, grads_ref, proj_ref, query_ref, length_ref, out_ref,
    rows, proj, query, sides, total, packed, spread, scores, parts,
    row_sem, proj_sem, query_sem,
    grad_send, grad_recv, score_send, score_recv,
):
    sec, dp = lax.axis_index("section"), lax.axis_index("dp")
    seq_len = inputs_ref.shape[2]
    step = inputs_ref.shape[3] // CHUNKS
    rank = proj_ref.shape[2] // 2
    block = query_ref.shape[1]
    group = members // sections
    per = width // block
    home = dp // group
    keeps = home == sec
    my_slot = (dp % group) // per * (sections * per) + sec * per + dp % per


    def chunk_copies(c):
        columns = pl.ds(pl.multiple_of(c * step, step), step)
        return (
            pltpu.make_async_copy(proj_ref.at[0, columns], proj.at[c], proj_sem.at[c]),
            pltpu.make_async_copy(
                inputs_ref.at[0, 0, :, columns], rows.at[c, pl.ds(0, seq_len)], row_sem.at[c, 0]
            ),
            pltpu.make_async_copy(
                grads_ref.at[0, 0, :, columns], rows.at[c, pl.ds(seq_len, seq_len)], row_sem.at[c, 1]
            ),
        )

    @pl.loop(0, CHUNKS)
    def _(c):
        for copy in chunk_copies(c):
            copy.start()

    query_copies = []
    for k in range(per):
        copy = pltpu.make_async_copy(query_ref.at[0], query.at[pl.ds(k * block, block)], query_sem.at[k])
        copy.start()
        query_copies.append(copy)

    barrier = pltpu.get_barrier_semaphore()

    @pl.loop(1, members)
    def _(k):
        pl.semaphore_signal(
            barrier, inc=1, device_id=(sec, lax.rem(dp + k, members)), device_id_type=MESH
        )

    @pl.loop(0, sections)
    def _(s):
        @pl.loop(0, group)
        def _(g):
            sender = sec * group + g

            @pl.when(jnp.logical_not(jnp.logical_and(s == sec, sender == dp)))
            def _():
                pl.semaphore_signal(barrier, inc=1, device_id=(s, sender), device_id_type=MESH)

    sides[...] = jnp.zeros_like(sides)

    @pl.loop(0, CHUNKS)
    def _(c):
        for copy in chunk_copies(c):
            copy.wait()
        sides[...] += lax.dot_general(
            proj[c].T, rows[c], (((1,), (1,)), ((), ())), preferred_element_type=jnp.float32
        )

    tokens = length_ref[0]
    slot = lax.broadcasted_iota(jnp.int32, (rank, seq_len), 1)
    grad_side = sides[pl.ds(rank, rank), pl.ds(seq_len, seq_len)]
    total[...] = lax.dot_general(
        jnp.where(slot < tokens, grad_side, 0.0).astype(jnp.bfloat16),
        sides[:, pl.ds(0, seq_len)].astype(jnp.bfloat16),
        (((1,), (1,)), ((), ())), preferred_element_type=jnp.float32,
    )
    half = rank // 2
    even = total[pl.ds(0, half, stride=2), :]
    odd = total[pl.ds(1, half, stride=2), :]
    lane = lax.broadcasted_iota(jnp.int32, (half, 2 * rank), 1)
    folded = jnp.where(lane < rank, even, pltpu.roll(odd, rank, 1))
    packed[dp] = (folded / tokens.astype(jnp.float32)).astype(jnp.bfloat16)

    pl.semaphore_wait(barrier, members - 1 + sections * group - jnp.where(keeps, 1, 0))

    def grad_copy(k):
        return pltpu.make_async_remote_copy(
            src_ref=packed.at[dp], dst_ref=packed.at[dp],
            send_sem=grad_send.at[k], recv_sem=grad_recv.at[k],
            device_id=(sec, lax.rem(dp + k, members)), device_id_type=MESH,
        )

    @pl.loop(1, members)
    def _(k):
        grad_copy(k).start()

    for copy in query_copies:
        copy.wait()

    @pl.loop(1, members)
    def _(k):
        grad_copy(k).wait_recv()

    spread[...] = packed[...].reshape(members * half, 2 * rank).astype(jnp.float32)
    left = jnp.concatenate(
        [spread[pl.ds(i, members, stride=half), :].astype(jnp.bfloat16) for i in range(half)], axis=1
    )
    found = lax.dot_general(
        left, query[...], (((1,), (1,)), ((), ())), preferred_element_type=jnp.float32
    )
    place = lax.broadcasted_iota(jnp.int32, found.shape, 1) // block
    found = jnp.where(place == dp % per, found, 0.0)
    scores[...] = found.reshape(members, 1, width)

    def score_copy(e):
        return pltpu.make_async_remote_copy(
            src_ref=scores.at[e], dst_ref=parts.at[my_slot],
            send_sem=score_send.at[e], recv_sem=score_recv.at[my_slot],
            device_id=(home, e), device_id_type=MESH,
        )

    @pl.loop(0, members)
    def _(k):
        e = lax.rem(dp + k, members)

        @pl.when(jnp.logical_or(jnp.logical_not(keeps), k > 0))
        def _():
            score_copy(e).start()

    @pl.when(keeps)
    def _():
        parts[my_slot] = scores[dp]

    @pl.loop(0, sections * group)
    def _(slot):
        @pl.when(jnp.logical_or(jnp.logical_not(keeps), slot != my_slot))
        def _():
            pltpu.make_async_remote_copy(
                src_ref=scores.at[0], dst_ref=parts.at[slot],
                send_sem=score_send.at[0], recv_sem=score_recv.at[slot],
                device_id=(home, dp), device_id_type=MESH,
            ).wait_recv()

    count = sections * per
    for b in range(group // per):
        piece = parts[b * count]
        for k in range(1, count):
            piece = piece + parts[b * count + k]
        out_ref[:, pl.ds(b * width, width)] = piece

    @pl.loop(1, members)
    def _(k):
        grad_copy(k).wait_send()

    @pl.loop(0, members)
    def _(k):
        @pl.when(jnp.logical_or(jnp.logical_not(keeps), k > 0))
        def _():
            score_copy(lax.rem(dp + k, members)).wait_send()


def solution(mesh):
    sections, members = mesh.shape["section"], mesh.shape["dp"]

    def on_device(layer_inputs, out_grads, projections, query_grads, lengths):
        seq_len, model_width = layer_inputs.shape[2:]
        rank = projections.shape[2] // 2
        block = query_grads.shape[1]
        flat = query_grads.shape[2]
        group = members // sections
        width = min(128, block * group)
        per = width // block
        half = rank // 2
        slots = sections * group
        step = model_width // CHUNKS
        held = [
            pltpu.with_memory_space_constraint(array, pltpu.HBM)
            for array in (layer_inputs, out_grads, projections, query_grads)
        ]
        return pl.pallas_call(
            functools.partial(kernel, sections, members, width),
            out_shape=jax.ShapeDtypeStruct((1, block * group), jnp.float32),
            in_specs=[pl.BlockSpec(memory_space=pltpu.HBM)] * 4 + [pl.BlockSpec(memory_space=pltpu.SMEM)],
            out_specs=pl.BlockSpec(memory_space=pltpu.VMEM),
            scratch_shapes=[
                pltpu.VMEM((CHUNKS, 2 * seq_len, step), jnp.bfloat16),
                pltpu.VMEM((CHUNKS, step, 2 * rank), jnp.bfloat16),
                pltpu.VMEM((width, flat), jnp.bfloat16),
                pltpu.VMEM((2 * rank, 2 * seq_len), jnp.float32),
                pltpu.VMEM((rank, 2 * rank), jnp.float32),
                pltpu.VMEM((members, half, 2 * rank), jnp.bfloat16),
                pltpu.VMEM((members * half, 2 * rank), jnp.float32),
                pltpu.VMEM((members, 1, width), jnp.float32),
                pltpu.VMEM((slots, 1, width), jnp.float32),
                pltpu.SemaphoreType.DMA((CHUNKS, 2)),
                pltpu.SemaphoreType.DMA((CHUNKS,)),
                pltpu.SemaphoreType.DMA((per,)),
                pltpu.SemaphoreType.DMA((members,)),
                pltpu.SemaphoreType.DMA((members,)),
                pltpu.SemaphoreType.DMA((members,)),
                pltpu.SemaphoreType.DMA((slots,)),
            ],
            compiler_params=pltpu.CompilerParams(
                collective_id=0, has_side_effects=True, vmem_limit_bytes=48 * 1024 * 1024
            ),
            cost_estimate=pl.CostEstimate(
                flops=8 * seq_len * model_width * rank,
                bytes_accessed=4 * seq_len * model_width,
                transcendentals=0,
            ),
        )(*held, lengths)

    placed = (
        P("section", "dp", None, None),
        P("section", "dp", None, None),
        P("section", None, None),
        P("section", "dp", None),
        P("dp"),
    )
    return jax.shard_map(
        on_device, mesh=mesh, in_specs=placed, out_specs=P("dp", "section"), check_vma=False
    )
```

```python
import functools

import jax
import jax.numpy as jnp
from jax import lax
from jax.experimental import pallas as pl
from jax.experimental.pallas import tpu as pltpu
from jax.sharding import PartitionSpec as P

MESH = pl.DeviceIdType.MESH
CHUNKS = 4


def kernel(
    sections, members, width,
    inputs_ref, grads_ref, proj_ref, query_ref, length_ref, out_ref,
    rows, proj, query, sides, total, packed, spread, scores, parts,
    row_sem, proj_sem, query_sem,
    grad_send, grad_recv, score_send, score_recv,
):
    sec, dp = lax.axis_index("section"), lax.axis_index("dp")
    seq_len = inputs_ref.shape[2]
    step = inputs_ref.shape[3] // CHUNKS
    rank = proj_ref.shape[2] // 2
    block = query_ref.shape[1]
    group = members // sections
    per = width // block
    home = dp // group
    keeps = home == sec
    my_slot = (dp % group) // per * (sections * per) + sec * per + dp % per


    def chunk_copies(c):
        columns = pl.ds(pl.multiple_of(c * step, step), step)
        return (
            pltpu.make_async_copy(proj_ref.at[0, columns], proj.at[c], proj_sem.at[c]),
            pltpu.make_async_copy(
                inputs_ref.at[0, 0, :, columns], rows.at[c, pl.ds(0, seq_len)], row_sem.at[c, 0]
            ),
            pltpu.make_async_copy(
                grads_ref.at[0, 0, :, columns], rows.at[c, pl.ds(seq_len, seq_len)], row_sem.at[c, 1]
            ),
        )

    @pl.loop(0, CHUNKS)
    def _(c):
        for copy in chunk_copies(c):
            copy.start()

    query_copies = []
    for k in range(per):
        copy = pltpu.make_async_copy(query_ref.at[0], query.at[pl.ds(k * block, block)], query_sem.at[k])
        copy.start()
        query_copies.append(copy)

    barrier = pltpu.get_barrier_semaphore()

    @pl.loop(1, members)
    def _(k):
        pl.semaphore_signal(
            barrier, inc=1, device_id=(sec, lax.rem(dp + k, members)), device_id_type=MESH
        )

    @pl.loop(0, sections)
    def _(s):
        @pl.loop(0, group)
        def _(g):
            sender = sec * group + g

            @pl.when(jnp.logical_not(jnp.logical_and(s == sec, sender == dp)))
            def _():
                pl.semaphore_signal(barrier, inc=1, device_id=(s, sender), device_id_type=MESH)

    sides[...] = jnp.zeros_like(sides)

    @pl.loop(0, CHUNKS)
    def _(c):
        for copy in chunk_copies(c):
            copy.wait()
        sides[...] += lax.dot_general(
            proj[c].T, rows[c], (((1,), (1,)), ((), ())), preferred_element_type=jnp.float32
        )

    tokens = length_ref[0]
    slot = lax.broadcasted_iota(jnp.int32, (rank, seq_len), 1)
    grad_side = sides[pl.ds(rank, rank), pl.ds(seq_len, seq_len)]
    total[...] = lax.dot_general(
        jnp.where(slot < tokens, grad_side, 0.0).astype(jnp.bfloat16),
        sides[:, pl.ds(0, seq_len)].astype(jnp.bfloat16),
        (((1,), (1,)), ((), ())), preferred_element_type=jnp.float32,
    )
    half = rank // 2
    even = total[pl.ds(0, half, stride=2), :]
    odd = total[pl.ds(1, half, stride=2), :]
    lane = lax.broadcasted_iota(jnp.int32, (half, 2 * rank), 1)
    folded = jnp.where(lane < rank, even, pltpu.roll(odd, rank, 1))
    packed[dp] = (folded / tokens.astype(jnp.float32)).astype(jnp.bfloat16)

    pl.semaphore_wait(barrier, members - 1 + sections * group - jnp.where(keeps, 1, 0))

    def grad_copy(k):
        return pltpu.make_async_remote_copy(
            src_ref=packed.at[dp], dst_ref=packed.at[dp],
            send_sem=grad_send.at[k], recv_sem=grad_recv.at[k],
            device_id=(sec, lax.rem(dp + k, members)), device_id_type=MESH,
        )

    @pl.loop(1, members)
    def _(k):
        grad_copy(k).start()

    for copy in query_copies:
        copy.wait()

    @pl.loop(1, members)
    def _(k):
        grad_copy(k).wait_recv()

    spread[...] = packed[...].reshape(members * half, 2 * rank).astype(jnp.float32)
    left = jnp.concatenate(
        [spread[pl.ds(i, members, stride=half), :].astype(jnp.bfloat16) for i in range(half)], axis=1
    )
    found = lax.dot_general(
        left, query[...], (((1,), (1,)), ((), ())), preferred_element_type=jnp.float32
    )
    place = lax.broadcasted_iota(jnp.int32, found.shape, 1) // block
    found = jnp.where(place == dp % per, found, 0.0)
    scores[...] = found.reshape(members, 1, width)

    def score_copy(e):
        return pltpu.make_async_remote_copy(
            src_ref=scores.at[e], dst_ref=parts.at[my_slot],
            send_sem=score_send.at[e], recv_sem=score_recv.at[my_slot],
            device_id=(home, e), device_id_type=MESH,
        )

    @pl.loop(0, members)
    def _(k):
        e = lax.rem(dp + k, members)

        @pl.when(jnp.logical_or(jnp.logical_not(keeps), k > 0))
        def _():
            score_copy(e).start()

    @pl.when(keeps)
    def _():
        parts[my_slot] = scores[dp]

    @pl.loop(0, sections * group)
    def _(slot):
        @pl.when(jnp.logical_or(jnp.logical_not(keeps), slot != my_slot))
        def _():
            pltpu.make_async_remote_copy(
                src_ref=scores.at[0], dst_ref=parts.at[slot],
                send_sem=score_send.at[0], recv_sem=score_recv.at[slot],
                device_id=(home, dp), device_id_type=MESH,
            ).wait_recv()

    count = sections * per
    for b in range(group // per):
        piece = parts[b * count]
        for k in range(1, count):
            piece = piece + parts[b * count + k]
        out_ref[:, pl.ds(b * width, width)] = piece

    @pl.loop(1, members)
    def _(k):
        grad_copy(k).wait_send()

    @pl.loop(0, members)
    def _(k):
        @pl.when(jnp.logical_or(jnp.logical_not(keeps), k > 0))
        def _():
            score_copy(lax.rem(dp + k, members)).wait_send()


def solution(mesh):
    sections, members = mesh.shape["section"], mesh.shape["dp"]

    def on_device(layer_inputs, out_grads, projections, query_grads, lengths):
        seq_len, model_width = layer_inputs.shape[2:]
        rank = projections.shape[2] // 2
        block = query_grads.shape[1]
        flat = query_grads.shape[2]
        group = members // sections
        width = min(128, block * group)
        per = width // block
        half = rank // 2
        slots = sections * group
        step = model_width // CHUNKS
        held = [
            pltpu.with_memory_space_constraint(array, pltpu.HBM)
            for array in (layer_inputs, out_grads, projections, query_grads)
        ]
        return pl.pallas_call(
            functools.partial(kernel, sections, members, width),
            out_shape=jax.ShapeDtypeStruct((1, block * group), jnp.float32),
            in_specs=[pl.BlockSpec(memory_space=pltpu.HBM)] * 4 + [pl.BlockSpec(memory_space=pltpu.SMEM)],
            out_specs=pl.BlockSpec(memory_space=pltpu.VMEM),
            scratch_shapes=[
                pltpu.VMEM((CHUNKS, 2 * seq_len, step), jnp.bfloat16),
                pltpu.VMEM((CHUNKS, step, 2 * rank), jnp.bfloat16),
                pltpu.VMEM((width, flat), jnp.bfloat16),
                pltpu.VMEM((2 * rank, 2 * seq_len), jnp.float32),
                pltpu.VMEM((rank, 2 * rank), jnp.float32),
                pltpu.VMEM((members, half, 2 * rank), jnp.bfloat16),
                pltpu.VMEM((members * half, 2 * rank), jnp.float32),
                pltpu.VMEM((members, 1, width), jnp.float32),
                pltpu.VMEM((slots, 1, width), jnp.float32),
                pltpu.SemaphoreType.DMA((CHUNKS, 2)),
                pltpu.SemaphoreType.DMA((CHUNKS,)),
                pltpu.SemaphoreType.DMA((per,)),
                pltpu.SemaphoreType.DMA((members,)),
                pltpu.SemaphoreType.DMA((members,)),
                pltpu.SemaphoreType.DMA((members,)),
                pltpu.SemaphoreType.DMA((slots,)),
            ],
            compiler_params=pltpu.CompilerParams(
                collective_id=0, has_side_effects=True, vmem_limit_bytes=48 * 1024 * 1024
            ),
            cost_estimate=pl.CostEstimate(
                flops=8 * seq_len * model_width * rank,
                bytes_accessed=4 * seq_len * model_width,
                transcendentals=0,
            ),
        )(*held, lengths)

    placed = (
        P("section", "dp", None, None),
        P("section", "dp", None, None),
        P("section", None, None),
        P("section", "dp", None),
        P("dp"),
    )
    return jax.shard_map(
        on_device, mesh=mesh, in_specs=placed, out_specs=P("dp", "section"), check_vma=False
    )
```
